32 devices in a mesh: dp: 4 (over z), wide: 8 (over y, x, core).
Axes of the slice: x: 2, y: 2, z: 4, core: 2. Of those that a mesh axis runs over, the one named last changes fastest.
Arguments:
- row_ids: int32 [32768, 2, 26], P(('dp', 'wide')), may hold values from 0 to 8191, as said below
- dense_in: float32 [32768, 13], P(('dp', 'wide')), may hold values from -16 to 16
- tables: bfloat16 [26, 262144, 16], P(None, ('dp', 'wide')), may hold values from -6 to 6
- cotangent: bfloat16 [32768, 768], P(('dp', 'wide')), may hold values from -8 to 8
- in_weight: float32 [6, 512, 256], P(None, 'wide'), may hold values from -0.25 to 0.25
- in_momentum: float32 [6, 512, 256], P(None, 'wide'), may hold values from -112 to 112
- in_average: float32 [6, 512, 256], P(None, 'wide'), may hold values from -0.25 to 0.25
- mid_weight: float32 [6, 256, 256], P(None, 'wide'), may hold values from -0.375 to 0.375
- mid_momentum: float32 [6, 256, 256], P(None, 'wide'), may hold values from -160 to 160
- mid_average: float32 [6, 256, 256], P(None, 'wide'), may hold values from -0.375 to 0.375
- norm_weight: float32 [6, 2, 256], P(None, None, 'wide'), may hold values from -1.5 to 1.5, as said below
- norm_momentum: float32 [6, 2, 256], P(None, None, 'wide'), may hold values from -320 to 320
- norm_average: float32 [6, 2, 256], P(None, None, 'wide'), may hold values from -1.5 to 1.5, as said below
- gate_weight: float32 [512, 14], P('wide'), may hold values from -0.25 to 0.25
- gate_momentum: float32 [512, 14], P('wide'), may hold values from -224 to 224
- gate_average: float32 [512, 14], P('wide'), may hold values from -0.25 to 0.25
- dense_weight: float32 [13, 96], P(None, 'wide'), may hold values from -1.75 to 1.75
- dense_momentum: float32 [13, 96], P(None, 'wide'), may hold values from -320 to 320
- dense_average: float32 [13, 96], P(None, 'wide'), may hold values from -1.75 to 1.75
Outputs:
- gate_outputs: bfloat16 [32768, 768], P(('dp', 'wide'))
- dense_grad: float32 [32768, 13], P(('dp', 'wide'))
- table_grad: float32 [26, 262144, 16], P(None, ('dp', 'wide'))
- new_in_weight: float32 [6, 512, 256], P(None, 'wide')
- new_in_momentum: float32 [6, 512, 256], P(None, 'wide')
- new_in_average: float32 [6, 512, 256], P(None, 'wide')
- new_mid_weight: float32 [6, 256, 256], P(None, 'wide')
- new_mid_momentum: float32 [6, 256, 256], P(None, 'wide')
- new_mid_average: float32 [6, 256, 256], P(None, 'wide')
- new_norm_weight: float32 [6, 2, 256], P(None, None, 'wide')
- new_norm_momentum: float32 [6, 2, 256], P(None, None, 'wide')
- new_norm_average: float32 [6, 2, 256], P(None, None, 'wide')
- new_gate_weight: float32 [512, 14], P('wide')
- new_gate_momentum: float32 [512, 14], P('wide')
- new_gate_average: float32 [512, 14], P('wide')
- new_dense_weight: float32 [13, 96], P(None, 'wide')
- new_dense_momentum: float32 [13, 96], P(None, 'wide')
- new_dense_average: float32 [13, 96], P(None, 'wide')
The draws below stay inside these ranges and needn't reach their ends.
Inputs may be any that keep to these rules, and one draw needn't show every extreme that they name: row_ids[e, 0, f] is a device index along dp+wide, from 0 to 31, and row_ids[e, 1, f] a row of that device, from 0 to 8191; the o-th device along dp+wide holds rows o * 8192 to (o + 1) * 8192 - 1 of every table. Of the lookups of one device's 1024 events (aligned blocks), at most 1248 fall on the rows of one device; in every draw one device receives exactly 1248 from every device. `norm_weight`: row 0 lies between 0.5 and 1.5. `norm_average`: row 0 lies between 0.5 and 1.5.
All inputs are finite; a program needn't handle non-finite values.
Results may differ from the reference program's by a relative error of at most 0.0097.
Values may be sent and summed in bfloat16 or wider, within the bound.
No kernel may reach another device: no remote copies, remote signals or barrier semaphores. Data moves between devices by JAX's collectives and lax.ppermute only.
A program may use at most 256 MiB of HBM per device.

```python
import math
import jax
import jax.numpy as jnp
from jax import lax

FIELDS = 26
EMB = 16
DENSE = 13
DENSE_OUT = 96
H = 256
EXPERTS = 6
ROWS_DEV = 8192
EV_DEV = 1024
D_IN = 512
EVENTS = 32768
ROWS = 262144
N_DP = 4
N_WIDE = 8


def draw_row_ids(key, part):
    key = jax.random.fold_in(key, 11)
    devices = N_DP * N_WIDE
    lookups = EV_DEV * FIELDS
    capacity = 3 * lookups // (2 * devices)
    hot_key, owner_key, place_key = jax.random.split(key, 3)
    hottest = jax.random.randint(hot_key, (), 0, devices)

    def one_device(dev_key):
        spread_key, shuffle_key, draw_key = jax.random.split(dev_key, 3)
        others = jax.random.permutation(spread_key, (devices - 1) * capacity)[:lookups - capacity]
        owners = jnp.concatenate([jnp.zeros((capacity,), jnp.int32), 1 + others // capacity])
        owners = (hottest + owners) % devices
        owners = jax.random.permutation(shuffle_key, owners)
        inverse = jax.random.randint(draw_key, (lookups,), 1, ROWS_DEV + 1)
        return (owners, inverse)
    owners, inverse = jax.vmap(one_device)(jax.random.split(owner_key, devices))
    shuffled = jax.random.permutation(place_key, ROWS_DEV).astype(jnp.int32)
    placing = (shuffled - shuffled[ROWS_DEV - 1] + ROWS_DEV - 1) % ROWS_DEV
    local = placing[ROWS_DEV // inverse - 1]
    owners = owners.reshape(EV_DEV * devices, FIELDS)
    local = local.reshape(EV_DEV * devices, FIELDS)
    return jnp.stack([owners, local], axis=1).astype(jnp.int32)


def draw_dense_in(key, part):
    key = jax.random.fold_in(key, 12)
    rows = EV_DEV * N_DP * N_WIDE
    base_key, shift_key = jax.random.split(key)
    place = jnp.arange(rows, dtype=jnp.float32) / rows
    base = jnp.clip(jax.random.normal(base_key, (rows, DENSE), jnp.float32), -4.0, 4.0)
    rising = 1.0 + 2.0 * place
    shift = jax.random.uniform(shift_key, (DENSE,), jnp.float32, -1.0, 1.0)
    return (base + 0.5) * rising[:, None] + shift[None, :]


def draw_cotangent(key, part):
    key = jax.random.fold_in(key, 13)
    rows = EV_DEV * N_DP * N_WIDE
    place = jnp.arange(rows, dtype=jnp.float32) / rows
    base = jnp.clip(jax.random.normal(key, (rows, 3 * H), jnp.float32), -4.0, 4.0)
    rising = 0.6 + 1.2 * place
    return (base * rising[:, None]).astype(jnp.bfloat16)


def norm_law(key, scale):
    gain_key, shift_key = jax.random.split(key)
    gain = jax.random.uniform(gain_key, (EXPERTS, 1, H), jnp.float32, 0.5, 1.5)
    shift = scale * jnp.clip(jax.random.normal(shift_key, (EXPERTS, 1, H), jnp.float32), -3.0, 3.0)
    return jnp.concatenate([gain, shift], axis=1)


def draw_norm_weight(key, part):
    key = jax.random.fold_in(key, 14)
    return norm_law(key, 0.3)


def draw_norm_average(key, part):
    key = jax.random.fold_in(key, 15)
    return norm_law(key, 0.3)


def levels(stream_key, dims, cuts, smallest, largest):
    def one(dim, shards_of):
        draws = jax.random.uniform(jax.random.fold_in(jax.random.fold_in(stream_key, 6), dim), (shards_of,), jnp.float32, smallest / len(cuts), largest / len(cuts))
        return jnp.repeat(jnp.exp(draws), dims[dim] // shards_of).reshape((-1,) + (1,) * (len(dims) - dim - 1))

    level = one(*cuts[0])
    for cut in cuts[1:]:
        level = level * one(*cut)
    return level


def centred(own_key, shape, scale, reach, cuts=(), held_as=jnp.bfloat16):
    level = levels(own_key, shape, cuts, -0.22, 0.18) if cuts else 1.0
    drawn = jax.random.normal(own_key, shape, jnp.float32) * scale * level
    return jnp.minimum(jnp.maximum(drawn, -reach), reach).astype(held_as)


def setup_inputs(seed: int = 0) -> dict:
    splits = jax.random.split(jax.random.key(seed), 20)
    row_ids = draw_row_ids(jax.random.fold_in(splits[19], 71), 0)
    dense_in = draw_dense_in(jax.random.fold_in(splits[19], 71), 0)
    tables = centred(splits[2], (FIELDS, ROWS, EMB), 1.0, 6.0, ((1, 32),))
    cotangent = draw_cotangent(jax.random.fold_in(splits[19], 71), 0)
    in_weight = centred(splits[4], (EXPERTS, D_IN, H), D_IN ** -0.5, 0.25, ((1, 8),), jnp.float32)
    in_momentum = centred(splits[5], (EXPERTS, D_IN, H), (0.1 * EVENTS ** 0.5), 112.0, ((1, 8),), jnp.float32)
    in_average = centred(splits[6], (EXPERTS, D_IN, H), D_IN ** -0.5, 0.25, ((1, 8),), jnp.float32)
    mid_weight = centred(splits[7], (EXPERTS, H, H), H ** -0.5, 0.375, ((1, 8),), jnp.float32)
    mid_momentum = centred(splits[8], (EXPERTS, H, H), (0.15 * EVENTS ** 0.5), 160.0, ((1, 8),), jnp.float32)
    mid_average = centred(splits[9], (EXPERTS, H, H), H ** -0.5, 0.375, ((1, 8),), jnp.float32)
    norm_weight = draw_norm_weight(jax.random.fold_in(splits[19], 71), 0)
    norm_momentum = centred(splits[11], (EXPERTS, 2, H), (0.3 * EVENTS ** 0.5), 320.0, ((2, 8),), jnp.float32)
    norm_average = draw_norm_average(jax.random.fold_in(splits[19], 71), 0)
    gate_weight = centred(splits[13], (D_IN, 14), D_IN ** -0.5, 0.25, ((0, 8),), jnp.float32)
    gate_momentum = centred(splits[14], (D_IN, 14), (0.2 * EVENTS ** 0.5), 224.0, ((0, 8),), jnp.float32)
    gate_average = centred(splits[15], (D_IN, 14), D_IN ** -0.5, 0.25, ((0, 8),), jnp.float32)
    dense_weight = centred(splits[16], (DENSE, DENSE_OUT), DENSE ** -0.5, 1.75, ((1, 8),), jnp.float32)
    dense_momentum = centred(splits[17], (DENSE, DENSE_OUT), (0.3 * EVENTS ** 0.5), 320.0, ((1, 8),), jnp.float32)
    dense_average = centred(splits[18], (DENSE, DENSE_OUT), DENSE ** -0.5, 1.75, ((1, 8),), jnp.float32)
    return dict(row_ids=row_ids, dense_in=dense_in, tables=tables, cotangent=cotangent, in_weight=in_weight, in_momentum=in_momentum, in_average=in_average, mid_weight=mid_weight, mid_momentum=mid_momentum, mid_average=mid_average, norm_weight=norm_weight, norm_momentum=norm_momentum, norm_average=norm_average, gate_weight=gate_weight, gate_momentum=gate_momentum, gate_average=gate_average, dense_weight=dense_weight, dense_momentum=dense_momentum, dense_average=dense_average)


EPS = 1e-05
MOMENTUM = 0.5
AVERAGE = 0.5
HIGH = lax.Precision.HIGHEST

@jax.custom_vjp
def low(v):
    return lax.optimization_barrier(v.astype(jnp.bfloat16)).astype(jnp.float32)

@jax.custom_vjp
def low_back(v):
    return v

def low_keep(v):
    return (low(v), None)

def low_pass(kept, grad):
    return (grad,)

def back_keep(v):
    return (v, None)

def back_low(kept, grad):
    return (low(grad),)
low.defvjp(low_keep, low_pass)
low_back.defvjp(back_keep, back_low)

def layer_norm(hidden, gain, shift):
    centre = hidden - lax.optimization_barrier(jnp.mean(hidden, axis=-1, keepdims=True))
    inv_std = lax.rsqrt(lax.optimization_barrier(jnp.mean(centre * centre, axis=-1, keepdims=True)) + EPS)
    return centre * inv_std * gain + shift

def mixing_of(logits):
    gate_a = jax.nn.softmax(logits[:, 0:4], axis=-1)
    gate_b = jax.nn.softmax(logits[:, 4:8], axis=-1)
    gate_s = jax.nn.softmax(logits[:, 8:14], axis=-1)
    blank = jnp.zeros_like(gate_a[:, 0:2])
    row_a = jnp.concatenate([gate_a[:, 0:2], blank, gate_a[:, 2:4]], axis=1)
    row_b = jnp.concatenate([blank, gate_b], axis=1)
    return jnp.stack([row_a, row_b, gate_s], axis=1)

def expert_block(features, in_low, mid_low, norm_low, gate_low):
    logits = low_back(jnp.dot(features, gate_low, precision=HIGH))
    mixing = mixing_of(logits)
    pre_in = low_back(jnp.einsum('bd,edh->ebh', features, in_low, precision=HIGH))
    hidden_in = low(jax.nn.gelu(pre_in))
    pre_mid = low_back(jnp.einsum('ebh,ehk->ebk', hidden_in, mid_low, precision=HIGH))
    hidden_mid = jax.nn.gelu(pre_mid)
    expert_out = layer_norm(hidden_mid, norm_low[:, 0:1, :], norm_low[:, 1:2, :])
    mixed = jnp.einsum('bge,ebh->bgh', mixing, expert_out, precision=HIGH)
    return mixed.reshape(mixed.shape[0], -1)

def forward(tables, dense_in, in_weight, mid_weight, norm_weight, gate_weight, dense_weight, row_ids):
    mean_dense = lax.optimization_barrier(jnp.mean(dense_in, axis=0))
    variance = lax.optimization_barrier(jnp.mean(dense_in * dense_in, axis=0)) - mean_dense * mean_dense
    normed = (dense_in - mean_dense) * lax.rsqrt(variance + EPS)
    projected = jnp.dot(normed, low(dense_weight), precision=HIGH)
    fields = row_ids.shape[2]
    row_of = (row_ids[:, 0, :] * ROWS_DEV + row_ids[:, 1, :]).astype(jnp.int32)
    looked = tables[jnp.arange(fields, dtype=jnp.int32)[None, :], row_of]
    looked = looked.reshape(row_ids.shape[0], -1)
    features = low(jnp.concatenate([looked, projected], axis=1))
    in_low = low(in_weight)
    mid_low = low(mid_weight)
    norm_low = low(norm_weight)
    gate_low = low(gate_weight)

    def one_block(block):
        return expert_block(block, in_low, mid_low, norm_low, gate_low)
    blocks = features.reshape(EVENTS // EV_DEV, EV_DEV, features.shape[1])
    outputs = lax.map(jax.checkpoint(one_block), blocks)
    return outputs.reshape(EVENTS, -1)

def update(weight, momentum, average, grad, rate):
    new_momentum = MOMENTUM * momentum + grad
    new_weight = weight - rate / math.sqrt(EVENTS) * (grad + MOMENTUM * new_momentum)
    new_average = AVERAGE * average + (1.0 - AVERAGE) * new_weight
    return (new_weight, new_momentum, new_average)

def reference(row_ids, dense_in, tables, cotangent, in_weight, in_momentum, in_average, mid_weight, mid_momentum, mid_average, norm_weight, norm_momentum, norm_average, gate_weight, gate_momentum, gate_average, dense_weight, dense_momentum, dense_average):

    def wrapped(tab, dense, w_in, w_mid, w_norm, w_gate, w_dense):
        return forward(tab, dense, w_in, w_mid, w_norm, w_gate, w_dense, row_ids)
    outputs, pull = jax.vjp(wrapped, tables.astype(jnp.float32), dense_in, in_weight, mid_weight, norm_weight, gate_weight, dense_weight)
    grads = pull(cotangent.astype(jnp.float32))
    new_in = update(in_weight, in_momentum, in_average, grads[2], 0.3)
    new_mid = update(mid_weight, mid_momentum, mid_average, grads[3], 0.3)
    new_norm = update(norm_weight, norm_momentum, norm_average, grads[4], 0.6)
    new_gate = update(gate_weight, gate_momentum, gate_average, grads[5], 0.15)
    new_dense = update(dense_weight, dense_momentum, dense_average, grads[6], 0.6)
    return (outputs.astype(jnp.bfloat16), grads[1], grads[0], new_in[0], new_in[1], new_in[2], new_mid[0], new_mid[1], new_mid[2], new_norm[0], new_norm[1], new_norm[2], new_gate[0], new_gate[1], new_gate[2], new_dense[0], new_dense[1], new_dense[2])
```

```python
import functools
import math

import jax
import jax.numpy as jnp
from jax import lax
from jax.experimental import pallas as pl
from jax.experimental.pallas import tpu as pltpu
from jax.sharding import PartitionSpec as P

EPS = 1e-05
MOMENTUM = 0.5
AVERAGE = 0.5
HIGH = lax.Precision.HIGHEST
LANES = 128
ROW_SPLIT = 512
VMEM_BYTES = 48 * 1024 * 1024


def layer_norm(hidden, gain, shift):
    centre = hidden - jnp.mean(hidden, axis=-1, keepdims=True)
    inv_std = lax.rsqrt(jnp.mean(centre * centre, axis=-1, keepdims=True) + EPS)
    normal = centre * inv_std
    return (normal * gain + shift, normal, inv_std)


def gelu_grad(preact, upstream):
    return jax.vjp(jax.nn.gelu, preact)[1](upstream)[0]


def softmax_back(probs, upstream):
    return probs * (upstream - jnp.sum(probs * upstream, axis=-1, keepdims=True))


def update(weight, momentum, average, grad, rate):
    new_momentum = MOMENTUM * momentum + grad
    new_weight = weight - rate * (grad + MOMENTUM * new_momentum)
    new_average = AVERAGE * average + (1.0 - AVERAGE) * new_weight
    return (new_weight, new_momentum, new_average)


def params(**kw):
    return pltpu.CompilerParams(vmem_limit_bytes=VMEM_BYTES, **kw)


def lane_ids(shape, dtype):
    return lax.broadcasted_iota(dtype, shape, len(shape) - 1)


def segment_parts(load, a, d, length, last_tile, lanes):
    am = a & (LANES - 1)
    dm = d & (LANES - 1)
    shift = (dm - am) & (LANES - 1)
    ta = lax.shift_right_logical(a, 7)
    r0 = pltpu.roll(load(jnp.minimum(ta, last_tile)), shift, 1)
    r1 = pltpu.roll(load(jnp.minimum(ta + 1, last_tile)), shift, 1)
    ahead = dm >= am
    kind = lanes.dtype
    cut0 = jnp.where(ahead, LANES, shift).astype(kind)
    cut1 = jnp.where(ahead, shift, 0).astype(kind)
    v0 = jnp.where(lanes < cut0, r0, r1)
    v1 = jnp.where(lanes < cut1, r0, r1)
    return dm, v0, v1


def move_short(load, store, segments, last_tile, last_dst, lanes, first):
    kind = lanes.dtype
    cur = first
    for a, d, length in segments:
        dm, v0, v1 = segment_parts(load, a, d, length, last_tile, lanes)
        cur = jnp.where(lanes >= dm.astype(kind), v0, cur)
        store(jnp.minimum(lax.shift_right_logical(d, 7), last_dst), cur)
        crossed = jnp.where(dm + length >= LANES, LANES, 0).astype(kind)
        cur = jnp.where(lanes < crossed, v1, cur)
    a, d, length = segments[-1]
    store(jnp.minimum(lax.shift_right_logical(d + length, 7), last_dst), cur)


def move_long(load, store, read, segment_at, count, last_tile, last_dst, lanes):
    kind = lanes.dtype

    def one(i, _):
        a, d, length = segment_at(i)

        def chunk(k, _):
            left = jnp.minimum(length - k * LANES, LANES)
            dk = d + k * LANES
            dm, v0, v1 = segment_parts(load, a + k * LANES, dk, left, last_tile, lanes)
            td = lax.shift_right_logical(dk, 7)
            low = dm.astype(kind)
            high = (dm + left).astype(kind)
            keep = (lanes >= low) & (lanes < high)
            store(td, jnp.where(keep, v0, read(td)))
            nxt = jnp.minimum(td + 1, last_dst)
            over = jnp.maximum(dm + left - LANES, 0).astype(kind)
            store(nxt, jnp.where(lanes < over, v1, read(nxt)))
            return 0

        lax.fori_loop(0, lax.shift_right_logical(length + LANES - 1, 7), chunk, 0)
        return 0

    lax.fori_loop(0, count, one, 0)


def move(load, store, read, segment_at, count, longest, last_tile, last_dst, lanes, blank):
    @pl.when(longest <= LANES)
    def _():
        if count <= 32:
            move_short(load, store, [segment_at(i) for i in range(count)], last_tile, last_dst, lanes, blank)
        else:
            step = 32
            assert count % step == 0

            def some(g, _):
                first = read(jnp.minimum(lax.shift_right_logical(segment_at(g * step)[1], 7), last_dst))
                move_short(load, store, [segment_at(g * step + i) for i in range(step)], last_tile, last_dst, lanes, first)
                return 0

            lax.fori_loop(0, count // step, some, 0)

    @pl.when(longest > LANES)
    def _():
        move_long(load, store, read, segment_at, count, last_tile, last_dst, lanes)


def row_load(ref, base=0):
    return lambda t: ref[pl.ds(base + t, 1), :]


def row_store(ref, base=0):
    def put(t, v):
        ref[pl.ds(base + t, 1), :] = v
    return put


def tile_load(ref, base=0):
    return lambda t: ref[base + t]


def tile_store(ref, base=0):
    def put(t, v):
        ref[base + t] = v
    return put


def request_kernel(fields, devices, tiles, start_ref, off_ref, cnt_ref, longest_ref, pos_ref, code_ref, counts_ref, out_ref, inv_ref, sorted_ref):
    f = pl.program_id(0)
    events = pos_ref.shape[2]
    ev_tiles = events // LANES
    code = code_ref[0]
    event = lane_ids((1, events), jnp.int32)
    sub = lax.broadcasted_iota(jnp.int32, (16, events), 0)
    rows = jnp.where(sub == 0, code >> 7, jnp.where(sub == 1, code & 127, jnp.where(sub == 2, event >> 7, jnp.where(sub == 3, event & 127, 0))))
    rows = rows.astype(jnp.float32).astype(jnp.bfloat16)
    place = pos_ref[0].astype(jnp.int16)
    for c in range(events // 256):
        ids = lax.broadcasted_iota(jnp.int16, (256, events), 0) + jnp.int16(c * 256)
        onehot = jnp.where(place == ids, jnp.bfloat16(1), jnp.bfloat16(0))
        got = lax.dot_general(rows, onehot, (((1,), (1,)), ((), ())), preferred_element_type=jnp.float32)
        got = got.astype(jnp.int32)
        value = got[0:1] * 128 + got[1:2]
        inverse = got[2:3] * 128 + got[3:4]
        inv_ref[0, :, c * 256:(c + 1) * 256] = inverse
        for h in range(2):
            sorted_ref[pl.ds(f * ev_tiles + c * 2 + h, 1), :] = value[:, h * 128:(h + 1) * 128]

    @pl.when(f == fields - 1)
    def _():
        lanes = lane_ids((1, LANES), jnp.int32)
        blank = jnp.zeros((1, LANES), jnp.int32)

        def owner(o, _):
            def segment_at(i):
                k = i * devices + o
                return start_ref[k] + i * events, off_ref[k], cnt_ref[k]

            move(row_load(sorted_ref), row_store(out_ref, o * tiles), row_load(out_ref, o * tiles), segment_at, fields, longest_ref[o],
                 fields * ev_tiles - 1, tiles - 1, lanes, blank)
            last = o * tiles + tiles - 1
            tail = out_ref[pl.ds(last, 1), :]
            out_ref[pl.ds(last, 1), :] = jnp.where(lanes >= LANES - fields, counts_ref[pl.ds(o, 1), :], tail)
            return 0

        lax.fori_loop(0, devices, owner, 0)


def build_request(start, off, cnt, longest, pos, code, counts, tiles):
    fields, events = pos.shape
    devices = counts.shape[0]
    kernel = functools.partial(request_kernel, fields, devices, tiles)
    return pl.pallas_call(
        kernel,
        grid_spec=pltpu.PrefetchScalarGridSpec(
            num_scalar_prefetch=4,
            grid=(fields,),
            in_specs=[
                pl.BlockSpec((1, 1, events), lambda f, *_: (f, 0, 0)),
                pl.BlockSpec((1, 1, events), lambda f, *_: (f, 0, 0)),
                pl.BlockSpec((devices, LANES), lambda f, *_: (0, 0)),
            ],
            out_specs=[
                pl.BlockSpec((devices * tiles, LANES), lambda f, *_: (0, 0)),
                pl.BlockSpec((1, 1, events), lambda f, *_: (f, 0, 0)),
            ],
            scratch_shapes=[pltpu.VMEM((fields * events // LANES, LANES), jnp.int32)],
        ),
        out_shape=[
            jax.ShapeDtypeStruct((devices * tiles, LANES), jnp.int32),
            jax.ShapeDtypeStruct((fields, 1, events), jnp.int32),
        ],
        compiler_params=params(),
        name="build_request",
    )(start, off, cnt, longest, pos.reshape(fields, 1, events), code.reshape(fields, 1, events), counts)


def fetch_kernel(fields, devices, tiles, soff_ref, fst_ref, cnt_ref, total_ref, base_ref, longf_ref, longs_ref, asked_ref, table_ref, out_ref, codes_ref, vals_ref):
    f = pl.program_id(0)
    rows_dev = table_ref.shape[2]
    parts = rows_dev // ROW_SPLIT
    slots = devices * tiles
    fm_tiles = codes_ref.shape[0]
    base = base_ref[f]
    lanes = lane_ids((1, LANES), jnp.int32)
    blank = jnp.zeros((1, LANES), jnp.int32)

    def segment_in(s):
        k = f * devices + s
        return soff_ref[k] + s * tiles * LANES, fst_ref[k] + base * LANES, cnt_ref[k]

    move(row_load(asked_ref), row_store(codes_ref), row_load(codes_ref), segment_in, devices, longf_ref[f], slots - 1, fm_tiles - 1, lanes, blank)

    stacked = jnp.concatenate([table_ref[0, :, p * ROW_SPLIT:(p + 1) * ROW_SPLIT] for p in range(parts)], axis=0)
    ids = lax.broadcasted_iota(jnp.int16, (ROW_SPLIT, 256), 0)

    def pair(t, _):
        at = base + 2 * t
        code = jnp.concatenate([codes_ref[pl.ds(at, 1), :], codes_ref[pl.ds(at + 1, 1), :]], axis=1)
        low = (code & (ROW_SPLIT - 1)).astype(jnp.int16)
        high = code >> 9
        onehot = jnp.where(low == ids, jnp.bfloat16(1), jnp.bfloat16(0))
        wide = jnp.dot(stacked, onehot, preferred_element_type=jnp.float32)
        got = jnp.zeros((16, 256), jnp.float32)
        for p in range(parts):
            got = jnp.where(high == p, wide[p * 16:(p + 1) * 16], got)
        got = got.astype(jnp.bfloat16)
        vals_ref[at] = got[:, :LANES]
        vals_ref[at + 1] = got[:, LANES:]
        return 0

    lax.fori_loop(0, lax.shift_right_logical(total_ref[f] + 255, 8), pair, 0)

    @pl.when(f == fields - 1)
    def _():
        lanes16 = lane_ids((16, LANES), jnp.int16)
        blank16 = jnp.zeros((16, LANES), jnp.bfloat16)

        def source(s, _):
            def segment_at(i):
                k = i * devices + s
                return fst_ref[k] + base_ref[i] * LANES, soff_ref[k], cnt_ref[k]

            move(tile_load(vals_ref), tile_store(out_ref, s * tiles), tile_load(out_ref, s * tiles), segment_at, fields, longs_ref[s],
                 fm_tiles - 1, tiles - 1, lanes16, blank16)
            return 0

        lax.fori_loop(0, devices, source, 0)


def fetch_rows(soff, fst, cnt, total, base, longf, longs, asked, tables_t, tiles, fm_tiles):
    fields, columns, rows_dev = tables_t.shape
    devices = asked.shape[0] // tiles
    kernel = functools.partial(fetch_kernel, fields, devices, tiles)
    return pl.pallas_call(
        kernel,
        grid_spec=pltpu.PrefetchScalarGridSpec(
            num_scalar_prefetch=7,
            grid=(fields,),
            in_specs=[
                pl.BlockSpec((devices * tiles, LANES), lambda f, *_: (0, 0)),
                pl.BlockSpec((1, columns, rows_dev), lambda f, *_: (f, 0, 0)),
            ],
            out_specs=[
                pl.BlockSpec((devices * tiles, columns, LANES), lambda f, *_: (0, 0, 0)),
                pl.BlockSpec((fm_tiles, LANES), lambda f, *_: (0, 0)),
            ],
            scratch_shapes=[pltpu.VMEM((fm_tiles, columns, LANES), jnp.bfloat16)],
        ),
        out_shape=[
            jax.ShapeDtypeStruct((devices * tiles, columns, LANES), jnp.bfloat16),
            jax.ShapeDtypeStruct((fm_tiles, LANES), jnp.int32),
        ],
        compiler_params=params(),
        name="fetch_rows",
    )(soff, fst, cnt, total, base, longf, longs, asked, tables_t)


def unsort_kernel(devices, tiles, start_ref, off_ref, cnt_ref, longest_ref, pos_ref, got_ref, out_ref, sorted_ref):
    f = pl.program_id(0)
    events = pos_ref.shape[2]
    ev_tiles = events // LANES
    lanes16 = lane_ids((16, LANES), jnp.int16)
    blank16 = jnp.zeros((16, LANES), jnp.bfloat16)

    def segment_at(o):
        k = f * devices + o
        return off_ref[k] + o * tiles * LANES, start_ref[k], cnt_ref[k]

    move(tile_load(got_ref), tile_store(sorted_ref), tile_load(sorted_ref), segment_at, devices, longest_ref[f], devices * tiles - 1, ev_tiles, lanes16, blank16)
    rows = jnp.concatenate([sorted_ref[t] for t in range(ev_tiles)], axis=1)
    for c in range(events // 256):
        place = pos_ref[0, :, c * 256:(c + 1) * 256].astype(jnp.int16)
        ids = lax.broadcasted_iota(jnp.int16, (events, 256), 0)
        onehot = jnp.where(place == ids, jnp.bfloat16(1), jnp.bfloat16(0))
        got = jnp.dot(rows, onehot, preferred_element_type=jnp.float32)
        out_ref[0, :, c * 256:(c + 1) * 256] = got.astype(jnp.bfloat16)


def unsort_rows(start, off, cnt, longest, pos, got, tiles):
    fields, events = pos.shape
    devices = got.shape[0] // tiles
    columns = got.shape[1]
    kernel = functools.partial(unsort_kernel, devices, tiles)
    return pl.pallas_call(
        kernel,
        grid_spec=pltpu.PrefetchScalarGridSpec(
            num_scalar_prefetch=4,
            grid=(fields,),
            in_specs=[
                pl.BlockSpec((1, 1, events), lambda f, *_: (f, 0, 0)),
                pl.BlockSpec((devices * tiles, columns, LANES), lambda f, *_: (0, 0, 0)),
            ],
            out_specs=pl.BlockSpec((1, columns, events), lambda f, *_: (f, 0, 0)),
            scratch_shapes=[pltpu.VMEM((events // LANES + 1, columns, LANES), jnp.bfloat16)],
        ),
        out_shape=jax.ShapeDtypeStruct((fields, columns, events), jnp.bfloat16),
        compiler_params=params(),
        name="unsort_rows",
    )(start, off, cnt, longest, pos.reshape(fields, 1, events), got)


def sort_kernel(fields, devices, tiles, start_ref, off_ref, cnt_ref, longest_ref, inv_ref, grad_ref, out_ref, sorted_ref):
    f = pl.program_id(0)
    events = inv_ref.shape[2]
    ev_tiles = events // LANES
    rows = grad_ref[0]
    for c in range(events // 256):
        place = inv_ref[0, :, c * 256:(c + 1) * 256].astype(jnp.int16)
        ids = lax.broadcasted_iota(jnp.int16, (events, 256), 0)
        onehot = jnp.where(place == ids, jnp.bfloat16(1), jnp.bfloat16(0))
        got = jnp.dot(rows, onehot, preferred_element_type=jnp.float32).astype(jnp.bfloat16)
        for h in range(2):
            sorted_ref[f * ev_tiles + c * 2 + h] = got[:, h * 128:(h + 1) * 128]

    @pl.when(f == fields - 1)
    def _():
        lanes16 = lane_ids((16, LANES), jnp.int16)
        blank16 = jnp.zeros((16, LANES), jnp.bfloat16)

        def owner(o, _):
            def segment_at(i):
                k = i * devices + o
                return start_ref[k] + i * events, off_ref[k], cnt_ref[k]

            move(tile_load(sorted_ref), tile_store(out_ref, o * tiles), tile_load(out_ref, o * tiles), segment_at, fields, longest_ref[o],
                 fields * ev_tiles - 1, tiles - 1, lanes16, blank16)
            return 0

        lax.fori_loop(0, devices, owner, 0)


def sort_grads(start, off, cnt, longest, inv, grads, tiles):
    fields, columns, events = grads.shape
    devices = start.shape[0] // fields
    kernel = functools.partial(sort_kernel, fields, devices, tiles)
    return pl.pallas_call(
        kernel,
        grid_spec=pltpu.PrefetchScalarGridSpec(
            num_scalar_prefetch=4,
            grid=(fields,),
            in_specs=[
                pl.BlockSpec((1, 1, events), lambda f, *_: (f, 0, 0)),
                pl.BlockSpec((1, columns, events), lambda f, *_: (f, 0, 0)),
            ],
            out_specs=pl.BlockSpec((devices * tiles, columns, LANES), lambda f, *_: (0, 0, 0)),
            scratch_shapes=[pltpu.VMEM((fields * events // LANES, columns, LANES), jnp.bfloat16)],
        ),
        out_shape=jax.ShapeDtypeStruct((devices * tiles, columns, LANES), jnp.bfloat16),
        compiler_params=params(),
        name="sort_grads",
    )(start, off, cnt, longest, inv, grads)


def add_kernel(fields, devices, tiles, soff_ref, fst_ref, cnt_ref, total_ref, base_ref, longf_ref, codes_ref, grads_ref, out_ref, vals_ref, sum_ref):
    f = pl.program_id(0)
    rows_dev = out_ref.shape[2]
    parts = rows_dev // ROW_SPLIT
    slots = devices * tiles
    base = base_ref[f]
    total = total_ref[f]
    lanes16 = lane_ids((16, LANES), jnp.int16)
    blank16 = jnp.zeros((16, LANES), jnp.bfloat16)

    def segment_in(s):
        k = f * devices + s
        return soff_ref[k] + s * tiles * LANES, fst_ref[k], cnt_ref[k]

    move(tile_load(grads_ref), tile_store(vals_ref), tile_load(vals_ref), segment_in, devices, longf_ref[f], slots - 1, vals_ref.shape[0] - 1, lanes16, blank16)
    ids = lax.broadcasted_iota(jnp.int16, (ROW_SPLIT, 256), 0)
    sum_ref[...] = jnp.zeros_like(sum_ref)

    def pair(t, _):
        at = base + 2 * t
        code = jnp.concatenate([codes_ref[pl.ds(at, 1), :], codes_ref[pl.ds(at + 1, 1), :]], axis=1)
        low = (code & (ROW_SPLIT - 1)).astype(jnp.int16)
        used = lane_ids((1, 256), jnp.int32) + t * 256 < total
        high = jnp.where(used, code >> 9, -1).astype(jnp.int16)
        onehot = jnp.where(low == ids, jnp.bfloat16(1), jnp.bfloat16(0))
        vals = jnp.concatenate([vals_ref[2 * t], vals_ref[2 * t + 1]], axis=1)
        high = jnp.broadcast_to(high, (16, 256))
        zero = jnp.zeros_like(vals)
        spread = jnp.concatenate([jnp.where(high == jnp.int16(p), vals, zero) for p in range(parts)], axis=0)
        sum_ref[...] += lax.dot_general(spread, onehot, (((1,), (1,)), ((), ())), preferred_element_type=jnp.float32)
        return 0

    lax.fori_loop(0, lax.shift_right_logical(total + 255, 8), pair, 0)
    for p in range(parts):
        out_ref[0, :, p * ROW_SPLIT:(p + 1) * ROW_SPLIT] = sum_ref[p * 16:(p + 1) * 16, :]


def add_grads(soff, fst, cnt, total, base, longf, codes, grads, tiles, fields, rows_dev):
    devices = grads.shape[0] // tiles
    columns = grads.shape[1]
    fm_tiles = codes.shape[0]
    kernel = functools.partial(add_kernel, fields, devices, tiles)
    return pl.pallas_call(
        kernel,
        grid_spec=pltpu.PrefetchScalarGridSpec(
            num_scalar_prefetch=6,
            grid=(fields,),
            in_specs=[
                pl.BlockSpec((fm_tiles, LANES), lambda f, *_: (0, 0)),
                pl.BlockSpec((devices * tiles, columns, LANES), lambda f, *_: (0, 0, 0)),
            ],
            out_specs=pl.BlockSpec((1, columns, rows_dev), lambda f, *_: (f, 0, 0)),
            scratch_shapes=[
                pltpu.VMEM((fm_tiles + 2, columns, LANES), jnp.bfloat16),
                pltpu.VMEM((rows_dev // ROW_SPLIT * columns, ROW_SPLIT), jnp.float32),
            ],
        ),
        out_shape=jax.ShapeDtypeStruct((fields, columns, rows_dev), jnp.float32),
        compiler_params=params(),
        name="add_grads",
    )(soff, fst, cnt, total, base, longf, codes, grads)


def local(
    row_ids,
    dense_in,
    tables,
    cotangent,
    in_weight,
    in_momentum,
    in_average,
    mid_weight,
    mid_momentum,
    mid_average,
    norm_weight,
    norm_momentum,
    norm_average,
    gate_weight,
    gate_momentum,
    gate_average,
    dense_weight,
    dense_momentum,
    dense_average,
):
    events = row_ids.shape[0]
    fields = row_ids.shape[2]
    rows_dev = tables.shape[1]
    columns = tables.shape[2]
    everyone = ("dp", "wide")
    devices = lax.axis_size(everyone)
    total_events = events * devices
    lookups = events * fields
    capacity = 3 * lookups // (2 * devices)
    tiles = -(-(capacity + fields) // LANES)
    fm_tiles = -(-devices * capacity // LANES) + 2 * fields + 2

    ids = jnp.transpose(row_ids, (2, 1, 0))
    owners, local_rows = ids[:, 0, :], ids[:, 1, :]
    owned = (owners[:, None, :] == jnp.arange(devices, dtype=jnp.int32)[None, :, None]).astype(jnp.bfloat16)
    steps = jnp.arange(events, dtype=jnp.int32)
    upper = (steps[:, None] < steps[None, :]).astype(jnp.bfloat16)
    before = jnp.einsum("fde,ex->fdx", owned, upper, preferred_element_type=jnp.float32)
    owned = owned.astype(jnp.float32)
    cnt = jnp.sum(owned, axis=2).astype(jnp.int32)
    start = jnp.cumsum(cnt, axis=1) - cnt
    off = jnp.cumsum(cnt, axis=0) - cnt
    pos = jnp.sum(owned * (before + start[:, :, None].astype(jnp.float32)), axis=1).astype(jnp.int32)
    counts = jnp.pad(cnt.T, ((0, 0), (LANES - fields, 0)))
    long_owner, long_field = jnp.max(cnt, axis=0), jnp.max(cnt, axis=1)
    start_s, off_s, cnt_s = start.reshape(-1), off.reshape(-1), cnt.reshape(-1)
    request, inverse = build_request(start_s, off_s, cnt_s, long_owner, pos, local_rows, counts, tiles)
    asked = lax.all_to_all(request.reshape(devices, tiles, LANES), everyone, split_axis=0, concat_axis=0, tiled=True)

    in_b, mid_b, norm_b, gate_b, dense_b = (
        lax.all_gather(in_weight.astype(jnp.bfloat16), "wide", axis=1, tiled=True),
        lax.all_gather(mid_weight.astype(jnp.bfloat16), "wide", axis=1, tiled=True),
        lax.all_gather(norm_weight.astype(jnp.bfloat16), "wide", axis=2, tiled=True),
        lax.all_gather(gate_weight.astype(jnp.bfloat16), "wide", axis=0, tiled=True),
        lax.all_gather(dense_weight.astype(jnp.bfloat16), "wide", axis=1, tiled=True),
    )
    sums = lax.psum(
        (jnp.sum(dense_in, axis=0), jnp.sum(dense_in * dense_in, axis=0)), ("dp", "wide")
    )
    mean_dense = sums[0] / total_events
    variance = sums[1] / total_events - mean_dense * mean_dense
    inv_dense = lax.rsqrt(variance + EPS)
    normed = (dense_in - mean_dense) * inv_dense
    dense_full = dense_b.astype(jnp.float32)
    projected = jnp.dot(normed, dense_full, precision=HIGH)

    got_cnt = asked[:, tiles - 1, LANES - fields:].T
    soff = jnp.cumsum(got_cnt, axis=0) - got_cnt
    fst = jnp.cumsum(got_cnt, axis=1) - got_cnt
    total = jnp.sum(got_cnt, axis=1)
    pairs = (total + 2 * LANES - 1) // (2 * LANES) * 2
    base = jnp.cumsum(pairs) - pairs
    long_source, long_in = jnp.max(got_cnt, axis=0), jnp.max(got_cnt, axis=1)
    soff_s, fst_s, got_s = soff.reshape(-1), fst.reshape(-1), got_cnt.reshape(-1)
    tables_t = jnp.transpose(tables, (0, 2, 1))
    fetched, codes = fetch_rows(
        soff_s, fst_s, got_s, total, base, long_in, long_source, asked.reshape(devices * tiles, LANES), tables_t, tiles, fm_tiles
    )
    returned = lax.all_to_all(fetched.reshape(devices, tiles, columns, LANES), everyone, split_axis=0, concat_axis=0, tiled=True)
    looked = unsort_rows(start_s, off_s, cnt_s, long_field, pos, returned.reshape(devices * tiles, columns, LANES), tiles)
    looked = looked.reshape(fields * columns, events).T
    features = jnp.concatenate([looked, projected.astype(jnp.bfloat16)], axis=1)
    logits = jnp.dot(features, gate_b, preferred_element_type=jnp.float32)
    gate_a = jax.nn.softmax(logits[:, 0:4], axis=-1)
    gate_bb = jax.nn.softmax(logits[:, 4:8], axis=-1)
    gate_s = jax.nn.softmax(logits[:, 8:14], axis=-1)
    blank = jnp.zeros_like(gate_a[:, 0:2])
    row_a = jnp.concatenate([gate_a[:, 0:2], blank, gate_a[:, 2:4]], axis=1)
    row_b = jnp.concatenate([blank, gate_bb], axis=1)
    mixing = jnp.stack([row_a, row_b, gate_s], axis=1)
    pre_in = jnp.einsum("bd,edh->ebh", features, in_b, preferred_element_type=jnp.float32)
    hidden_in = jax.nn.gelu(pre_in).astype(jnp.bfloat16)
    pre_mid = jnp.einsum("ebh,ehk->ebk", hidden_in, mid_b, preferred_element_type=jnp.float32)
    hidden_mid = jax.nn.gelu(pre_mid)
    norm_full = norm_b.astype(jnp.float32)
    gain = norm_full[:, 0:1, :]
    expert_out, normal, inv_std = layer_norm(hidden_mid, gain, norm_full[:, 1:2, :])
    mixed = jnp.einsum("bge,ebh->bgh", mixing, expert_out, precision=HIGH)
    gate_outputs = mixed.reshape(events, -1).astype(jnp.bfloat16)
    upstream = cotangent.astype(jnp.float32).reshape(events, 3, -1)
    d_out = jnp.einsum("bge,bgh->ebh", mixing, upstream, precision=HIGH)
    d_mixing = jnp.einsum("bgh,ebh->bge", upstream, expert_out, precision=HIGH)
    grad_a = softmax_back(
        gate_a, jnp.concatenate([d_mixing[:, 0, 0:2], d_mixing[:, 0, 4:6]], axis=1)
    )
    grad_b = softmax_back(gate_bb, d_mixing[:, 1, 2:6])
    grad_s = softmax_back(gate_s, d_mixing[:, 2, :])
    d_logits = jnp.concatenate([grad_a, grad_b, grad_s], axis=1).astype(jnp.bfloat16)
    norm_grad = jnp.stack([jnp.sum(d_out * normal, axis=1), jnp.sum(d_out, axis=1)], axis=1)
    d_norm = d_out * gain
    d_mid = inv_std * (
        d_norm
        - jnp.mean(d_norm, axis=-1, keepdims=True)
        - normal * jnp.mean(d_norm * normal, axis=-1, keepdims=True)
    )
    d_pre_mid = gelu_grad(pre_mid, d_mid).astype(jnp.bfloat16)
    mid_grad = jnp.einsum("ebh,ebk->ehk", hidden_in, d_pre_mid, preferred_element_type=jnp.float32)
    d_hidden = jnp.einsum("ebk,ehk->ebh", d_pre_mid, mid_b, preferred_element_type=jnp.float32)
    d_pre_in = gelu_grad(pre_in, d_hidden).astype(jnp.bfloat16)
    in_grad = jnp.einsum("bd,ebh->edh", features, d_pre_in, preferred_element_type=jnp.float32)
    gate_grad = jnp.einsum("bd,bk->dk", features, d_logits, preferred_element_type=jnp.float32)
    d_features = jnp.einsum("ebh,edh->bd", d_pre_in, in_b, preferred_element_type=jnp.float32)
    d_features = d_features + jnp.einsum(
        "bk,dk->bd", d_logits, gate_b, preferred_element_type=jnp.float32
    )
    d_looked = d_features[:, : fields * columns]
    d_projected = d_features[:, fields * columns :]
    dense_grad_w = jnp.einsum("bi,bo->io", normed, d_projected, precision=HIGH)
    d_normed = jnp.einsum("bo,io->bi", d_projected, dense_full, precision=HIGH)
    d_looked = d_looked.astype(jnp.bfloat16).T.reshape(fields, columns, events)
    outgoing = sort_grads(start_s, off_s, cnt_s, long_owner, inverse, d_looked, tiles)
    arrived = lax.all_to_all(outgoing.reshape(devices, tiles, columns, LANES), everyone, split_axis=0, concat_axis=0, tiled=True)
    table_grad = add_grads(
        soff_s, fst_s, got_s, total, base, long_in, codes, arrived.reshape(devices * tiles, columns, LANES), tiles, fields, rows_dev
    )
    table_grad = jnp.transpose(table_grad, (0, 2, 1))
    back_sum = jnp.sum(d_normed, axis=0)
    back_cross = jnp.sum(d_normed * normed, axis=0)
    shards = (
        lax.psum_scatter(in_grad, "wide", scatter_dimension=1, tiled=True),
        lax.psum_scatter(mid_grad, "wide", scatter_dimension=1, tiled=True),
        lax.psum_scatter(norm_grad, "wide", scatter_dimension=2, tiled=True),
        lax.psum_scatter(gate_grad, "wide", scatter_dimension=0, tiled=True),
        lax.psum_scatter(dense_grad_w, "wide", scatter_dimension=1, tiled=True),
    )
    grads = lax.psum((shards[0], shards[1], shards[2], shards[3], shards[4]), "dp")
    total_sum, total_cross = lax.psum((back_sum, back_cross), ("dp", "wide"))
    dense_grad = inv_dense * (
        d_normed - total_sum / total_events - normed * total_cross / total_events
    )
    scale = 1.0 / math.sqrt(total_events)
    new_in = update(in_weight, in_momentum, in_average, grads[0], 0.3 * scale)
    new_mid = update(mid_weight, mid_momentum, mid_average, grads[1], 0.3 * scale)
    new_norm = update(norm_weight, norm_momentum, norm_average, grads[2], 0.6 * scale)
    new_gate = update(gate_weight, gate_momentum, gate_average, grads[3], 0.15 * scale)
    new_dense = update(dense_weight, dense_momentum, dense_average, grads[4], 0.6 * scale)
    return (
        gate_outputs,
        dense_grad,
        table_grad,
        new_in[0],
        new_in[1],
        new_in[2],
        new_mid[0],
        new_mid[1],
        new_mid[2],
        new_norm[0],
        new_norm[1],
        new_norm[2],
        new_gate[0],
        new_gate[1],
        new_gate[2],
        new_dense[0],
        new_dense[1],
        new_dense[2],
    )


def solution(mesh):
    return jax.shard_map(
        local,
        mesh=mesh,
        in_specs=(
            P(("dp", "wide"), None, None),
            P(("dp", "wide"), None),
            P(None, ("dp", "wide"), None),
            P(("dp", "wide"), None),
            P(None, "wide", None),
            P(None, "wide", None),
            P(None, "wide", None),
            P(None, "wide", None),
            P(None, "wide", None),
            P(None, "wide", None),
            P(None, None, "wide"),
            P(None, None, "wide"),
            P(None, None, "wide"),
            P("wide", None),
            P("wide", None),
            P("wide", None),
            P(None, "wide"),
            P(None, "wide"),
            P(None, "wide"),
        ),
        out_specs=(
            P(("dp", "wide"), None),
            P(("dp", "wide"), None),
            P(None, ("dp", "wide"), None),
            P(None, "wide", None),
            P(None, "wide", None),
            P(None, "wide", None),
            P(None, "wide", None),
            P(None, "wide", None),
            P(None, "wide", None),
            P(None, None, "wide"),
            P(None, None, "wide"),
            P(None, None, "wide"),
            P("wide", None),
            P("wide", None),
            P("wide", None),
            P(None, "wide"),
            P(None, "wide"),
            P(None, "wide"),
        ),
        check_vma=False,
    )
```
